256 devices in a mesh: wide: 16 (over x, y_lo, core), deep: 16 (over z, y_hi).
Axes of the slice: x: 4, y: 4 (y_hi: 2, y_lo: 2; y = y_hi * 2 + y_lo), z: 8, core: 2. Of those that a mesh axis runs over, the one named last changes fastest.
Arguments:
- ratings: bfloat16 [131072, 4096], P(('wide', 'deep')), may hold values from -6 to 6
- recency_caps: int32 [131072, 8], P(('wide', 'deep')), may hold values from 1 to 512
- user_factors: float32 [131072, 256], P(('wide', 'deep')), may hold values from -0.75 to 0.75
- item_factors: float32 [131072, 256], P(('wide', 'deep')), may hold values from -0.75 to 0.75
- refresh_ids: int32 [32768], P(('wide', 'deep')), may hold values from 0 to 511
Outputs:
- users_out: float32 [131072, 256], P(('wide', 'deep'))
- items_out: float32 [131072, 256], P(('wide', 'deep'))
- scores: float32 [16, 2048, 8192], P('deep', None, 'wide')
The draws below stay inside these ranges and needn't reach their ends.
Inputs may be any that keep to these rules, and one draw needn't show every extreme that they name: `recency_caps`: an item of a block counts as rated by a user in that stratum when its recency position is below the user's cap. `refresh_ids`: indices into the device's own 512 users; repeats may occur.
All inputs are finite; a program needn't handle non-finite values.
Results may differ from the reference program's by a relative error of at most 0.0003.
Values sent between devices are 32-bit elements; how exact they have to be, the bound alone decides.
A program may use at most 64 MiB of HBM per device.

```python
import jax
import jax.numpy as jnp
from jax import lax

RANK = 256
BLOCK = 512
USERS = 512
REFRESH = 128
STRATA = 8
ALL_USERS = 131072
ALL_ITEMS = 131072
N_WIDE = 16
N_DEEP = 16


def factor_table(key, rows):
    return jnp.clip(0.25 * jax.random.normal(key, (rows, RANK), jnp.float32), -0.75, 0.75)


def draw_user_factors(key, part):
    key = jax.random.fold_in(key, 11)
    return factor_table(key, USERS * N_WIDE * N_DEEP)


def draw_item_factors(key, part):
    key = jax.random.fold_in(key, 23)
    return factor_table(key, BLOCK * N_WIDE * N_DEEP)


def plant(result, own_key, low, largest):
    longest = result.shape.index(max(result.shape))
    spots = []
    for shift in (0, 1):
        where = [jax.random.randint(jax.random.fold_in(own_key, axis), (), 0, length) for axis, length in enumerate(result.shape)]
        where[longest] = (where[longest] + shift) % result.shape[longest]
        spots.append(tuple(where))
    return result.at[spots[0]].set(low).at[spots[1]].set(largest)


def block_scale(stream_key, dims, pieces, smallest, high):
    factor_of = 1.0
    for position, parts in pieces:
        draws = jax.random.uniform(jax.random.fold_in(jax.random.fold_in(stream_key, 6), position), (parts,), jnp.float32, smallest / len(pieces), high / len(pieces))
        factor_of = factor_of * jnp.repeat(jnp.exp(draws), dims[position] // parts).reshape((-1,) + (1,) * (len(dims) - 1 - position))
    return factor_of


def bell_draw(stream_key, shape, scale, bound, pieces=(), kind=jnp.bfloat16):
    drawn = scale * jax.random.normal(stream_key, shape, jnp.float32)
    if pieces:
        drawn = drawn * block_scale(stream_key, shape, pieces, -0.22, 0.18)
    return jnp.clip(drawn, -bound, bound).astype(kind)


def setup_inputs(seed: int = 0) -> dict:
    seeds = jax.random.split(jax.random.key(seed), 6)
    return {
        "ratings": bell_draw(seeds[0], (ALL_USERS, STRATA * BLOCK), 1.0, 6.0, ((0, 256),)),
        "recency_caps": plant(jax.random.randint(seeds[1], (ALL_USERS, STRATA), 1, BLOCK + 1), jax.random.fold_in(seeds[1], 1), 1, BLOCK).astype(jnp.int32),
        "user_factors": draw_user_factors(jax.random.fold_in(seeds[5], 71), 0),
        "item_factors": draw_item_factors(jax.random.fold_in(seeds[5], 71), 0),
        "refresh_ids": plant(jax.random.randint(seeds[4], (N_WIDE * N_DEEP * REFRESH,), 0, USERS), jax.random.fold_in(seeds[4], 1), 0, USERS - 1).astype(jnp.int32),
    }


learn_rate = 0.1
penalty = 0.05

def update_pair(packed):
    user_rows, item_rows, rating_block, cap_column, confidence = packed
    predict = jnp.dot(user_rows, item_rows.T, precision=lax.Precision.HIGHEST)
    positions = lax.broadcasted_iota(jnp.int32, (1, BLOCK), 1)
    allowed = positions < cap_column[:, None]
    weighted = jnp.where(allowed, predict - rating_block.astype(jnp.float32), 0.0) * confidence[:, None]
    user_next = user_rows - learn_rate * (jnp.dot(weighted, item_rows, precision=lax.Precision.HIGHEST) + penalty * user_rows)
    item_next = item_rows - learn_rate * (jnp.dot(weighted.T, user_rows, precision=lax.Precision.HIGHEST) + penalty * item_rows)
    return (user_next, item_next)

def reference(ratings, recency_caps, user_factors, item_factors, refresh_ids):
    device_count = N_WIDE * N_DEEP
    user_blocks = user_factors.reshape(device_count, USERS, RANK)
    item_blocks = item_factors.reshape(device_count, BLOCK, RANK)
    rating_grid = ratings.reshape(device_count, USERS, STRATA, BLOCK)
    cap_grid = recency_caps.reshape(device_count, USERS, STRATA)
    counts = lax.optimization_barrier(jnp.sum(cap_grid, axis=2)).astype(jnp.float32)
    confidence = lax.rsqrt(counts)
    for stratum in range(STRATA):
        user_blocks, item_blocks = lax.map(update_pair, (user_blocks, item_blocks, rating_grid[:, :, stratum, :], cap_grid[:, :, stratum], confidence))
        item_blocks = jnp.roll(item_blocks, 1, axis=0)
    chosen_ids = refresh_ids.reshape(device_count, REFRESH)
    selected = jax.vmap(lambda table, picks: jnp.take(table, picks, axis=0))(user_blocks, chosen_ids)
    selected = selected.reshape(N_WIDE, N_DEEP, REFRESH, RANK)
    parked = item_blocks.reshape(N_WIDE, N_DEEP, BLOCK, RANK)

    def score_deep(index):
        left = lax.dynamic_index_in_dim(selected, index, 1, keepdims=False).reshape(N_WIDE * REFRESH, RANK)
        right = lax.dynamic_index_in_dim(parked, index, 1, keepdims=False).reshape(N_WIDE * BLOCK, RANK)
        return jnp.dot(left, right.T, precision=lax.Precision.HIGHEST)
    scores = lax.map(score_deep, jnp.arange(N_DEEP, dtype=jnp.int32))
    return (user_blocks.reshape(ALL_USERS, RANK), item_blocks.reshape(ALL_ITEMS, RANK), scores)
```

```python
import functools

import jax
import jax.numpy as jnp
from jax import lax
from jax.experimental import pallas as pl
from jax.experimental.pallas import tpu as pltpu
from jax.sharding import PartitionSpec as P

STRATA = 8
USERS = 512
BLOCK = 512
RANK = 256
REFRESH = 128
N_WIDE = 16
N_DEEP = 16
X = 4
CHUNKS = 4
C = BLOCK // CHUNKS

VMEM_BYTES = 60 * 2**20

learn_rate = 0.1
penalty = 0.05

MESH = pl.DeviceIdType.MESH
F32 = jnp.float32
BF16 = jnp.bfloat16


def split(value):
    high = value.astype(BF16)
    return high, (value - high.astype(F32)).astype(BF16)


def product(left, right, dims):
    numbers = ((dims[0], dims[1]), ((), ()))
    dot = functools.partial(lax.dot_general, dimension_numbers=numbers, preferred_element_type=F32)
    return dot(left[0], right[0]) + (dot(left[0], right[1]) + dot(left[1], right[0]))


def strata_kernel(
    ratings, caps_in, users_in, items_in, ids,
    users_out, items_out, picked_out,
    rated, caps_across, caps, users, users_high, users_low, gradient, held, leaving, picked, limit, confidence,
    load_sem, rated_sem, item_send, item_recv, pick_send, pick_recv, store_sem,
):
    wide, deep = lax.axis_index("wide"), lax.axis_index("deep")
    joined = wide * N_DEEP + deep
    after = lax.rem(joined + 1, N_WIDE * N_DEEP)
    before = lax.rem(joined + N_WIDE * N_DEEP - 1, N_WIDE * N_DEEP)
    after = (after // N_DEEP, lax.rem(after, N_DEEP))
    before = (before // N_DEEP, lax.rem(before, N_DEEP))

    x, y_low, core = wide // 4, lax.rem(wide // 2, 2), lax.rem(wide, 2)

    def place(x_by, y_flip, core_flip):
        return lax.rem(x + x_by, X) * 4 + (1 - y_low if y_flip else y_low) * 2 + (1 - core if core_flip else core)

    other_core = (place(0, False, True), deep)
    other_y = (place(0, True, False), deep)
    x_up = (place(1, False, False), deep)
    x_down = (place(3, False, False), deep)

    barrier = pltpu.get_barrier_semaphore()
    for peer in (after, before, other_core, other_y, x_up, x_down):
        pl.semaphore_signal(barrier, inc=1, device_id=peer, device_id_type=MESH)

    loads = [
        pltpu.make_async_copy(users_in, users, load_sem.at[0]),
        pltpu.make_async_copy(items_in, held.at[0], load_sem.at[1]),
        pltpu.make_async_copy(caps_in, caps_across, load_sem.at[2]),
    ]
    for load in loads:
        load.start()

    def rated_load(stratum):
        columns = pl.ds(pl.multiple_of(stratum * BLOCK, BLOCK), BLOCK)
        return pltpu.make_async_copy(ratings.at[:, columns], rated.at[stratum], rated_sem.at[stratum])

    for stratum in range(STRATA):
        rated_load(stratum).start()

    def item_copy(stratum, chunk):
        rows = pl.ds(chunk * C, C)
        return pltpu.make_async_remote_copy(
            src_ref=leaving.at[stratum, rows],
            dst_ref=held.at[stratum + 1, rows],
            send_sem=item_send.at[stratum, chunk],
            recv_sem=item_recv.at[stratum, chunk],
            device_id=after,
            device_id_type=MESH,
        )

    def prepare(stratum):
        lane = lax.broadcasted_iota(jnp.int32, (USERS, STRATA), 1)
        column = jnp.sum(jnp.where(lane == stratum, caps[...], 0), axis=1, keepdims=True)
        limit[...] = jnp.broadcast_to(column, (USERS, C))

    loads[2].wait()
    caps[...] = caps_across[...].T
    counts = jnp.sum(caps[...], axis=1, keepdims=True).astype(F32)
    confidence[...] = jnp.broadcast_to(lax.rsqrt(counts), (USERS, C))
    loads[0].wait()
    users_high[...], users_low[...] = split(users[...])
    loads[1].wait()

    pl.semaphore_wait(barrier, 6)

    def one_stratum(stratum, carry):
        prepare(stratum)
        rated_load(stratum).wait()
        for chunk in range(CHUNKS):

            @pl.when(stratum > 0)
            def _():
                item_copy(stratum - 1, chunk).wait_recv()

            rows = pl.ds(chunk * C, C)
            items = held[stratum, rows, :]
            items_pair = split(items)
            users_pair = (users_high[...], users_low[...])
            predict = product(users_pair, items_pair, ((1,), (1,)))
            block = rated[stratum, :, rows].astype(F32)
            position = lax.broadcasted_iota(jnp.int32, (USERS, C), 1) + chunk * C
            weighted = jnp.where(position < limit[...], predict - block, 0.0) * confidence[...]
            weighted_pair = split(weighted)
            change = product(weighted_pair, users_pair, ((0,), (0,)))
            leaving[stratum, rows, :] = items - learn_rate * (change + penalty * items)
            item_copy(stratum, chunk).start()
            part = product(weighted_pair, items_pair, ((1,), (0,)))
            gradient[...] = part if chunk == 0 else gradient[...] + part
        old = users[...]
        new = old - learn_rate * (gradient[...] + penalty * old)
        users[...] = new
        users_high[...], users_low[...] = split(new)
        return carry

    lax.fori_loop(0, STRATA, one_stratum, 0)

    stores = []

    def store(source, target):
        copy = pltpu.make_async_copy(source, target, store_sem.at[len(stores)])
        copy.start()
        stores.append(copy)

    new = users[...]
    high, rest = users_high[...], new - users_high[...].astype(F32)
    middle = rest.astype(BF16)
    low = (rest - middle.astype(F32)).astype(BF16)
    chosen = (lax.broadcasted_iota(jnp.int32, (USERS, REFRESH), 0) == ids[...]).astype(F32).astype(BF16)
    pick = functools.partial(
        lax.dot_general, chosen, dimension_numbers=(((0,), (0,)), ((), ())), preferred_element_type=F32
    )
    picked[wide] = pick(high) + (pick(middle) + pick(low))

    sent = []

    def give(slot, kind, peer, half=None):
        rows = pl.ds(0, REFRESH) if half is None else pl.ds(half * (REFRESH // 2), REFRESH // 2)
        copy = pltpu.make_async_remote_copy(
            src_ref=picked.at[slot, rows],
            dst_ref=picked.at[slot, rows],
            send_sem=pick_send.at[len(sent)],
            recv_sem=pick_recv.at[kind],
            device_id=peer,
            device_id_type=MESH,
        )
        copy.start()
        sent.append(copy)

    def take(slot, kind, half=None):
        rows = pl.ds(0, REFRESH) if half is None else pl.ds(half * (REFRESH // 2), REFRESH // 2)
        pltpu.make_async_remote_copy(
            src_ref=picked.at[slot, rows],
            dst_ref=picked.at[slot, rows],
            send_sem=pick_send.at[0],
            recv_sem=pick_recv.at[kind],
            device_id=other_core,
            device_id_type=MESH,
        ).wait_recv()

    def keep(slot):
        store(picked.at[slot], picked_out.at[pl.ds(pl.multiple_of(slot * REFRESH, REFRESH), REFRESH)])

    OTHER_Y, FROM_DOWN, FROM_UP, HALF_DOWN, HALF_UP, CORE = 0, 1, 3, 5, 7, 9
    give(wide, OTHER_Y, other_y)
    give(wide, FROM_DOWN, x_up)
    give(wide, FROM_UP, x_down)
    give(wide, CORE, other_core)
    store(users, users_out)
    keep(wide)

    slot = place(0, True, False)
    take(slot, OTHER_Y)
    give(slot, FROM_DOWN + 1, x_up)
    give(slot, FROM_UP + 1, x_down)
    give(slot, CORE + 1, other_core)
    keep(slot)

    for v in (0, 1):
        down, up = place(3, v == 1, False), place(1, v == 1, False)
        take(down, FROM_DOWN + v)
        give(down, HALF_DOWN + v, x_up, half=0)
        give(down, CORE + 2 + v, other_core)
        keep(down)
        take(up, FROM_UP + v)
        give(up, HALF_UP + v, x_down, half=1)
        give(up, CORE + 4 + v, other_core)
        keep(up)

    for v in (0, 1):
        far = place(2, v == 1, False)
        take(far, HALF_DOWN + v, half=0)
        take(far, HALF_UP + v, half=1)
        give(far, CORE + 6 + v, other_core)
        keep(far)

    for order, slot in enumerate(
        (
            place(0, False, True), place(0, True, True),
            place(3, False, True), place(3, True, True),
            place(1, False, True), place(1, True, True),
            place(2, False, True), place(2, True, True),
        )
    ):
        take(slot, CORE + order)
        keep(slot)

    for chunk in range(CHUNKS):
        rows = pl.ds(chunk * C, C)
        item_copy(STRATA - 1, chunk).wait_recv()
        store(held.at[STRATA, rows], items_out.at[rows])

    def drain(stratum, carry):
        for chunk in range(CHUNKS):
            item_copy(stratum, chunk).wait_send()
        return carry

    lax.fori_loop(0, STRATA, drain, 0)
    for copy in sent:
        copy.wait_send()
    for copy in stores:
        copy.wait()


def run_strata(ratings, caps, users, items, ids):
    sends, kinds, stores = 4 + 3 + 8 + 2, 17, 1 + 16 + CHUNKS
    anywhere = pl.BlockSpec(memory_space=pl.ANY)
    return pl.pallas_call(
        strata_kernel,
        out_shape=(
            jax.ShapeDtypeStruct((USERS, RANK), F32),
            jax.ShapeDtypeStruct((BLOCK, RANK), F32),
            jax.ShapeDtypeStruct((N_WIDE * REFRESH, RANK), F32),
        ),
        in_specs=[anywhere, anywhere, anywhere, anywhere, pl.BlockSpec(memory_space=pltpu.VMEM)],
        out_specs=(anywhere, anywhere, anywhere),
        scratch_shapes=[
            pltpu.VMEM((STRATA, USERS, BLOCK), BF16),
            pltpu.VMEM((STRATA, USERS), jnp.int32),
            pltpu.VMEM((USERS, STRATA), jnp.int32),
            pltpu.VMEM((USERS, RANK), F32),
            pltpu.VMEM((USERS, RANK), BF16),
            pltpu.VMEM((USERS, RANK), BF16),
            pltpu.VMEM((USERS, RANK), F32),
            pltpu.VMEM((STRATA + 1, BLOCK, RANK), F32),
            pltpu.VMEM((STRATA, BLOCK, RANK), F32),
            pltpu.VMEM((N_WIDE, REFRESH, RANK), F32),
            pltpu.VMEM((USERS, C), jnp.int32),
            pltpu.VMEM((USERS, C), F32),
            pltpu.SemaphoreType.DMA((3,)),
            pltpu.SemaphoreType.DMA((STRATA,)),
            pltpu.SemaphoreType.DMA((STRATA, CHUNKS)),
            pltpu.SemaphoreType.DMA((STRATA, CHUNKS)),
            pltpu.SemaphoreType.DMA((sends,)),
            pltpu.SemaphoreType.DMA((kinds,)),
            pltpu.SemaphoreType.DMA((stores,)),
        ],
        compiler_params=pltpu.CompilerParams(
            collective_id=0, has_side_effects=True, vmem_limit_bytes=VMEM_BYTES
        ),
    )(ratings, caps, users, items, ids)


def scores_kernel(picked, items, users_part, items_part, scores, users_out, items_out, items_high, items_low):
    @pl.when(pl.program_id(0) == 0)
    def _():
        items_high[...], items_low[...] = split(items[...])

    scores[...] = product(split(picked[...]), (items_high[...], items_low[...]), ((1,), (1,)))
    users_out[...] = users_part[...]
    items_out[...] = items_part[...]


def run_scores(picked, users, items):
    steps = 8
    rows = N_WIDE * REFRESH // steps
    part = pl.BlockSpec((USERS // steps, RANK), lambda i: (i, 0))
    return pl.pallas_call(
        scores_kernel,
        grid=(steps,),
        out_shape=(
            jax.ShapeDtypeStruct((N_WIDE * REFRESH, BLOCK), F32),
            jax.ShapeDtypeStruct((USERS, RANK), F32),
            jax.ShapeDtypeStruct((BLOCK, RANK), F32),
        ),
        in_specs=[
            pl.BlockSpec((rows, RANK), lambda i: (i, 0)),
            pl.BlockSpec((BLOCK, RANK), lambda i: (0, 0)),
            part,
            part,
        ],
        out_specs=(pl.BlockSpec((rows, BLOCK), lambda i: (i, 0)), part, part),
        scratch_shapes=[pltpu.VMEM((BLOCK, RANK), BF16), pltpu.VMEM((BLOCK, RANK), BF16)],
    )(picked, items, users, items)


def per_device(ratings, recency_caps, user_factors, item_factors, refresh_ids):
    users, items, picked = run_strata(
        ratings, recency_caps.T, user_factors, item_factors, refresh_ids.reshape(1, REFRESH)
    )
    scores, users, items = run_scores(picked, users, items)
    return (users, items, scores[None])


def solution(mesh):
    placed = (
        P(("wide", "deep"), None),
        P(("wide", "deep"), None),
        P(("wide", "deep"), None),
        P(("wide", "deep"), None),
        P(("wide", "deep")),
    )
    return jax.shard_map(
        per_device,
        mesh=mesh,
        in_specs=placed,
        out_specs=(P(("wide", "deep"), None), P(("wide", "deep"), None), P("deep", None, "wide")),
        check_vma=False,
    )
```

```python
import functools

import jax
import jax.numpy as jnp
from jax import lax
from jax.experimental import pallas as pl
from jax.experimental.pallas import tpu as pltpu
from jax.sharding import PartitionSpec as P

STRATA = 8
USERS = 512
BLOCK = 512
RANK = 256
REFRESH = 128
N_WIDE = 16
N_DEEP = 16
X = 4
CHUNKS = 4
C = BLOCK // CHUNKS

VMEM_BYTES = 44 * 2**20
PARTS = 4
HOLD = 2
HALF = REFRESH // 2
PART_ROWS = N_WIDE * REFRESH // PARTS

learn_rate = 0.1
penalty = 0.05

MESH = pl.DeviceIdType.MESH
F32 = jnp.float32
BF16 = jnp.bfloat16


def split(value):
    high = value.astype(BF16)
    return high, (value - high.astype(F32)).astype(BF16)


def product(left, right, dims):
    numbers = ((dims[0], dims[1]), ((), ()))
    dot = functools.partial(lax.dot_general, dimension_numbers=numbers, preferred_element_type=F32)
    return dot(left[0], right[0]) + (dot(left[0], right[1]) + dot(left[1], right[0]))


def strata_kernel(
    ratings, caps_in, users_in, items_in, ids,
    users_out, items_out, picked,
    rated, caps_across, caps, users, users_high, users_low, gradient, held, leaving, chosen, limit, confidence,
    load_sem, rated_sem, item_send, item_recv, last_recv, pick_send, pick_recv,
):
    wide, deep = lax.axis_index("wide"), lax.axis_index("deep")
    joined = wide * N_DEEP + deep
    after = lax.rem(joined + 1, N_WIDE * N_DEEP)
    before = lax.rem(joined + N_WIDE * N_DEEP - 1, N_WIDE * N_DEEP)
    after = (after // N_DEEP, lax.rem(after, N_DEEP))
    before = (before // N_DEEP, lax.rem(before, N_DEEP))

    x, y_low, core = wide // 4, lax.rem(wide // 2, 2), lax.rem(wide, 2)

    def place(x_by, y_flip, core_flip):
        return lax.rem(x + x_by, X) * 4 + (1 - y_low if y_flip else y_low) * 2 + (1 - core if core_flip else core)

    other_core = (place(0, False, True), deep)
    other_y = (place(0, True, False), deep)
    x_up = (place(1, False, False), deep)
    x_down = (place(3, False, False), deep)

    barrier = pltpu.get_barrier_semaphore()
    for peer in (after, before, other_core, other_y, x_up, x_down):
        pl.semaphore_signal(barrier, inc=1, device_id=peer, device_id_type=MESH)

    loads = [
        pltpu.make_async_copy(users_in, users, load_sem.at[0]),
        pltpu.make_async_copy(items_in, held.at[0], load_sem.at[1]),
        pltpu.make_async_copy(caps_in, caps_across, load_sem.at[2]),
    ]
    for load in loads:
        load.start()

    def rated_load(stratum):
        columns = pl.ds(pl.multiple_of(stratum * BLOCK, BLOCK), BLOCK)
        return pltpu.make_async_copy(ratings.at[:, columns], rated.at[stratum], rated_sem.at[stratum])

    for stratum in range(STRATA):
        rated_load(stratum).start()

    def item_copy(stratum, chunk):
        rows = pl.ds(chunk * C, C)
        return pltpu.make_async_remote_copy(
            src_ref=leaving.at[stratum, rows],
            dst_ref=held.at[stratum + 1, rows],
            send_sem=item_send.at[stratum, chunk],
            recv_sem=item_recv.at[stratum, chunk],
            device_id=after,
            device_id_type=MESH,
        )

    def last_item_copy(chunk):
        rows = pl.ds(chunk * C, C)
        return pltpu.make_async_remote_copy(
            src_ref=leaving.at[STRATA - 1, rows],
            dst_ref=items_out.at[rows],
            send_sem=item_send.at[STRATA - 1, chunk],
            recv_sem=last_recv.at[chunk],
            device_id=after,
            device_id_type=MESH,
        )

    def prepare(stratum):
        lane = lax.broadcasted_iota(jnp.int32, (USERS, STRATA), 1)
        column = jnp.sum(jnp.where(lane == stratum, caps[...], 0), axis=1, keepdims=True)
        limit[...] = jnp.broadcast_to(column, (USERS, C))

    loads[2].wait()
    caps[...] = caps_across[...].T
    counts = jnp.sum(caps[...], axis=1, keepdims=True).astype(F32)
    confidence[...] = jnp.broadcast_to(lax.rsqrt(counts), (USERS, C))
    loads[0].wait()
    users_high[...], users_low[...] = split(users[...])
    loads[1].wait()

    row = lax.broadcasted_iota(jnp.int32, (USERS, REFRESH), 0)
    chosen[...] = (row == ids[...]).astype(F32).T.astype(BF16)
    prepare(0)
    pl.semaphore_wait(barrier, 6)

    def weigh(stratum, chunk):
        rows = pl.ds(chunk * C, C)
        items_pair = split(held[stratum, rows, :])
        predict = product((users_high[...], users_low[...]), items_pair, ((1,), (1,)))
        block = rated[stratum, :, rows].astype(F32)
        position = lax.broadcasted_iota(jnp.int32, (USERS, C), 1) + chunk * C
        weighted = jnp.where(position < limit[...], predict - block, 0.0) * confidence[...]
        return split(weighted), items_pair

    def update_items(stratum, chunk, weighted_pair, users_pair):
        rows = pl.ds(chunk * C, C)
        items = held[stratum, rows, :]
        change = product(weighted_pair, users_pair, ((0,), (0,)))
        leaving[stratum, rows, :] = items - learn_rate * (change + penalty * items)

    def add_gradient(chunk, weighted_pair, items_pair):
        part = product(weighted_pair, items_pair, ((1,), (0,)))
        gradient[...] = part if chunk == 0 else gradient[...] + part

    def next_users():
        old = users[...]
        return old - learn_rate * (gradient[...] + penalty * old)

    def one_stratum(stratum, carry):
        rated_load(stratum).wait()
        for chunk in range(CHUNKS):

            @pl.when(stratum > 0)
            def _():
                item_copy(stratum - 1, chunk).wait_recv()

            weighted_pair, items_pair = weigh(stratum, chunk)
            update_items(stratum, chunk, weighted_pair, (users_high[...], users_low[...]))
            item_copy(stratum, chunk).start()
            add_gradient(chunk, weighted_pair, items_pair)
        new = next_users()
        users[...] = new
        users_high[...], users_low[...] = split(new)
        prepare(stratum + 1)
        return carry

    lax.fori_loop(0, STRATA - 1, one_stratum, 0)

    final = STRATA - 1
    rated_load(final).wait()
    waiting = []
    for chunk in range(CHUNKS):
        item_copy(final - 1, chunk).wait_recv()
        weighted_pair, items_pair = weigh(final, chunk)
        if chunk < CHUNKS - HOLD:
            update_items(final, chunk, weighted_pair, (users_high[...], users_low[...]))
            last_item_copy(chunk).start()
        else:
            waiting.append((chunk, weighted_pair))
        add_gradient(chunk, weighted_pair, items_pair)
    new = next_users()
    high, low = split(new)
    lowest = (new - high.astype(F32) - low.astype(F32)).astype(BF16)
    pick = functools.partial(lax.dot_general, dimension_numbers=(((1,), (0,)), ((), ())), preferred_element_type=F32)
    picked[wide] = pick(chosen[...], high) + (pick(chosen[...], low) + pick(chosen[...], lowest))

    sent = []

    def piece(slot, half):
        return picked.at[slot] if half is None else picked.at[slot, pl.ds(half * HALF, HALF)]

    def move(slot, half, kind, peer, number):
        return pltpu.make_async_remote_copy(
            src_ref=piece(slot, half),
            dst_ref=piece(slot, half),
            send_sem=pick_send.at[number],
            recv_sem=pick_recv.at[kind],
            device_id=peer,
            device_id_type=MESH,
        )

    def give(slot, half, kind, peer):
        copy = move(slot, half, kind, peer, len(sent))
        copy.start()
        sent.append(copy)

    def take(slot, half, kind):
        move(slot, half, kind, other_core, 0).wait_recv()

    def other_y_kind(half):
        return half

    def near_kind(v, from_up, half):
        return 2 + (v * 2 + from_up) * 2 + half

    def far_kind(v, half):
        return 10 + v * 2 + half

    def core_kind(order):
        return 14 + order

    for half in (0, 1):
        give(wide, half, other_y_kind(half), other_y)
        give(wide, half, near_kind(0, 0, half), x_up)
        give(wide, half, near_kind(0, 1, half), x_down)
    give(wide, None, core_kind(0), other_core)

    for chunk, weighted_pair in waiting:
        update_items(final, chunk, weighted_pair, (users_high[...], users_low[...]))
        last_item_copy(chunk).start()
    users_out[...] = new

    beside = place(0, True, False)
    down, up = place(3, False, False), place(1, False, False)
    beside_down, beside_up = place(3, True, False), place(1, True, False)
    for half in (0, 1):
        take(beside, half, other_y_kind(half))
        give(beside, half, near_kind(1, 0, half), x_up)
        give(beside, half, near_kind(1, 1, half), x_down)
        take(down, half, near_kind(0, 0, half))
        if half == 0:
            give(down, 0, far_kind(0, 0), x_up)
        take(up, half, near_kind(0, 1, half))
        if half == 1:
            give(up, 1, far_kind(0, 1), x_down)
    give(beside, None, core_kind(1), other_core)
    give(down, None, core_kind(2), other_core)
    give(up, None, core_kind(3), other_core)
    for half in (0, 1):
        take(beside_down, half, near_kind(1, 0, half))
        if half == 0:
            give(beside_down, 0, far_kind(1, 0), x_up)
        take(beside_up, half, near_kind(1, 1, half))
        if half == 1:
            give(beside_up, 1, far_kind(1, 1), x_down)
    give(beside_down, None, core_kind(4), other_core)
    give(beside_up, None, core_kind(5), other_core)
    for v in (0, 1):
        opposite = place(2, v == 1, False)
        for half in (0, 1):
            take(opposite, half, far_kind(v, half))
            give(opposite, half, core_kind(6 + 2 * v + half), other_core)

    for chunk in range(CHUNKS):
        last_item_copy(chunk).wait_recv()

    for order, slot in enumerate(
        (
            place(0, False, True), place(0, True, True),
            place(3, False, True), place(1, False, True),
            place(3, True, True), place(1, True, True),
        )
    ):
        take(slot, None, core_kind(order))
    for v in (0, 1):
        for half in (0, 1):
            take(place(2, v == 1, True), half, core_kind(6 + 2 * v + half))

    def drain(stratum, carry):
        for chunk in range(CHUNKS):
            item_copy(stratum, chunk).wait_send()
        return carry

    lax.fori_loop(0, STRATA - 1, drain, 0)
    for chunk in range(CHUNKS):
        last_item_copy(chunk).wait_send()
    for copy in sent:
        copy.wait_send()


def run_strata(ratings, caps, users, items, ids):
    sends, kinds = 27, 24
    far, here = pl.BlockSpec(memory_space=pltpu.HBM), pl.BlockSpec(memory_space=pltpu.VMEM)
    return pl.pallas_call(
        strata_kernel,
        out_shape=(
            jax.ShapeDtypeStruct((USERS, RANK), F32),
            jax.ShapeDtypeStruct((BLOCK, RANK), F32),
            jax.ShapeDtypeStruct((N_WIDE, REFRESH, RANK), F32),
        ),
        in_specs=[far, far, far, far, here],
        out_specs=(here, here, here),
        scratch_shapes=[
            pltpu.VMEM((STRATA, USERS, BLOCK), BF16),
            pltpu.VMEM((STRATA, USERS), jnp.int32),
            pltpu.VMEM((USERS, STRATA), jnp.int32),
            pltpu.VMEM((USERS, RANK), F32),
            pltpu.VMEM((USERS, RANK), BF16),
            pltpu.VMEM((USERS, RANK), BF16),
            pltpu.VMEM((USERS, RANK), F32),
            pltpu.VMEM((STRATA, BLOCK, RANK), F32),
            pltpu.VMEM((STRATA, BLOCK, RANK), F32),
            pltpu.VMEM((REFRESH, USERS), BF16),
            pltpu.VMEM((USERS, C), jnp.int32),
            pltpu.VMEM((USERS, C), F32),
            pltpu.SemaphoreType.DMA((3,)),
            pltpu.SemaphoreType.DMA((STRATA,)),
            pltpu.SemaphoreType.DMA((STRATA, CHUNKS)),
            pltpu.SemaphoreType.DMA((STRATA - 1, CHUNKS)),
            pltpu.SemaphoreType.DMA((CHUNKS,)),
            pltpu.SemaphoreType.DMA((sends,)),
            pltpu.SemaphoreType.DMA((kinds,)),
        ],
        compiler_params=pltpu.CompilerParams(
            collective_id=0, has_side_effects=True, vmem_limit_bytes=VMEM_BYTES
        ),
    )(ratings, caps, users, items, ids)


def scores_kernel(picked, items, users, scores, users_out, items_out, right, staged, store_sem):
    passed = [
        pltpu.make_async_copy(users, users_out, store_sem.at[0]),
        pltpu.make_async_copy(items, items_out, store_sem.at[1]),
    ]
    for copy in passed:
        copy.start()
    high, low = split(items[...].T)
    right[0:RANK, :], right[RANK : 2 * RANK, :], right[2 * RANK :, :] = high, low, high
    stores = []
    for part in range(PARTS):
        rows = pl.ds(part * PART_ROWS, PART_ROWS)
        high, low = split(picked[rows, :])
        left = jnp.concatenate([high, high, low], axis=1)
        staged[rows, :] = jnp.dot(left, right[...], preferred_element_type=F32)
        copy = pltpu.make_async_copy(staged.at[rows], scores.at[rows], store_sem.at[2 + part])
        copy.start()
        stores.append(copy)
    for copy in passed + stores:
        copy.wait()


def run_scores(picked, users, items):
    here = pl.BlockSpec(memory_space=pltpu.VMEM)
    anywhere = pl.BlockSpec(memory_space=pl.ANY)
    return pl.pallas_call(
        scores_kernel,
        out_shape=(
            jax.ShapeDtypeStruct((N_WIDE * REFRESH, BLOCK), F32),
            jax.ShapeDtypeStruct((USERS, RANK), F32),
            jax.ShapeDtypeStruct((BLOCK, RANK), F32),
        ),
        in_specs=[here, here, here],
        out_specs=(anywhere, anywhere, anywhere),
        scratch_shapes=[
            pltpu.VMEM((3 * RANK, BLOCK), BF16),
            pltpu.VMEM((N_WIDE * REFRESH, BLOCK), F32),
            pltpu.SemaphoreType.DMA((2 + PARTS,)),
        ],
        compiler_params=pltpu.CompilerParams(vmem_limit_bytes=32 * 2**20),
    )(picked, items, users)


def per_device(ratings, recency_caps, user_factors, item_factors, refresh_ids):
    inputs = (ratings, recency_caps.T, user_factors, item_factors, refresh_ids.reshape(1, REFRESH))
    inputs = [pltpu.with_memory_space_constraint(value, pltpu.HBM) for value in inputs]
    users, items, picked = run_strata(*inputs)
    scores, users, items = run_scores(picked.reshape(N_WIDE * REFRESH, RANK), users, items)
    return (users, items, scores[None])


def solution(mesh):
    placed = (
        P(("wide", "deep"), None),
        P(("wide", "deep"), None),
        P(("wide", "deep"), None),
        P(("wide", "deep"), None),
        P(("wide", "deep")),
    )
    return jax.shard_map(
        per_device,
        mesh=mesh,
        in_specs=placed,
        out_specs=(P(("wide", "deep"), None), P(("wide", "deep"), None), P("deep", None, "wide")),
        check_vma=False,
    )
```

```python
import functools

import jax
import jax.numpy as jnp
from jax import lax
from jax.experimental import pallas as pl
from jax.experimental.pallas import tpu as pltpu
from jax.sharding import PartitionSpec as P

STRATA = 8
USERS = 512
BLOCK = 512
RANK = 256
REFRESH = 128
N_WIDE = 16
N_DEEP = 16
X = 4
CHUNKS = 4
C = BLOCK // CHUNKS

VMEM_BYTES = 44 * 2**20
PARTS = 4
HOLD = 2
HALF = REFRESH // 2
PART_ROWS = N_WIDE * REFRESH // PARTS

learn_rate = 0.1
penalty = 0.05

MESH = pl.DeviceIdType.MESH
F32 = jnp.float32
BF16 = jnp.bfloat16


def split(value):
    high = value.astype(BF16)
    return high, (value - high.astype(F32)).astype(BF16)


def product(left, right, dims):
    numbers = ((dims[0], dims[1]), ((), ()))
    dot = functools.partial(lax.dot_general, dimension_numbers=numbers, preferred_element_type=F32)
    return dot(left[0], right[0]) + (dot(left[0], right[1]) + dot(left[1], right[0]))


def strata_kernel(
    ratings, caps_in, users_in, items_in, ids,
    users_out, items_out, picked,
    rated, caps_across, caps, users, users_high, users_low, gradient, held, leaving, chosen, limit, confidence,
    load_sem, rated_sem, item_send, item_recv, last_recv, pick_send, pick_recv,
):
    wide, deep = lax.axis_index("wide"), lax.axis_index("deep")
    joined = wide * N_DEEP + deep
    after = lax.rem(joined + 1, N_WIDE * N_DEEP)
    before = lax.rem(joined + N_WIDE * N_DEEP - 1, N_WIDE * N_DEEP)
    after = (after // N_DEEP, lax.rem(after, N_DEEP))
    before = (before // N_DEEP, lax.rem(before, N_DEEP))

    x, y_low, core = wide // 4, lax.rem(wide // 2, 2), lax.rem(wide, 2)

    def place(x_by, y_flip, core_flip):
        return lax.rem(x + x_by, X) * 4 + (1 - y_low if y_flip else y_low) * 2 + (1 - core if core_flip else core)

    other_core = (place(0, False, True), deep)
    other_y = (place(0, True, False), deep)
    x_up = (place(1, False, False), deep)
    x_down = (place(3, False, False), deep)

    barrier = pltpu.get_barrier_semaphore()
    for peer in (after, before, other_core, other_y, x_up, x_down):
        pl.semaphore_signal(barrier, inc=1, device_id=peer, device_id_type=MESH)

    loads = [
        pltpu.make_async_copy(users_in, users, load_sem.at[0]),
        pltpu.make_async_copy(items_in, held.at[0], load_sem.at[1]),
        pltpu.make_async_copy(caps_in, caps_across, load_sem.at[2]),
    ]
    for load in loads:
        load.start()

    def rated_load(stratum):
        columns = pl.ds(pl.multiple_of(stratum * BLOCK, BLOCK), BLOCK)
        return pltpu.make_async_copy(ratings.at[:, columns], rated.at[stratum], rated_sem.at[stratum])

    rated_load(0).start()

    def item_copy(stratum, chunk):
        rows = pl.ds(chunk * C, C)
        return pltpu.make_async_remote_copy(
            src_ref=leaving.at[stratum, rows],
            dst_ref=held.at[stratum + 1, rows],
            send_sem=item_send.at[stratum, chunk],
            recv_sem=item_recv.at[stratum, chunk],
            device_id=after,
            device_id_type=MESH,
        )

    def last_item_copy(chunk):
        rows = pl.ds(chunk * C, C)
        return pltpu.make_async_remote_copy(
            src_ref=leaving.at[STRATA - 1, rows],
            dst_ref=items_out.at[rows],
            send_sem=item_send.at[STRATA - 1, chunk],
            recv_sem=last_recv.at[chunk],
            device_id=after,
            device_id_type=MESH,
        )

    def prepare(stratum):
        lane = lax.broadcasted_iota(jnp.int32, (USERS, STRATA), 1)
        column = jnp.sum(jnp.where(lane == stratum, caps[...], 0), axis=1, keepdims=True)
        limit[...] = jnp.broadcast_to(column, (USERS, C))

    loads[2].wait()
    caps[...] = caps_across[...].T
    counts = jnp.sum(caps[...], axis=1, keepdims=True).astype(F32)
    confidence[...] = jnp.broadcast_to(lax.rsqrt(counts), (USERS, C))
    loads[0].wait()
    users_high[...], users_low[...] = split(users[...])
    loads[1].wait()

    prepare(0)
    pl.semaphore_wait(barrier, 6)

    def weigh(stratum, chunk):
        rows = pl.ds(chunk * C, C)
        items_pair = split(held[stratum, rows, :])
        predict = product((users_high[...], users_low[...]), items_pair, ((1,), (1,)))
        block = rated[stratum, :, rows].astype(F32)
        position = lax.broadcasted_iota(jnp.int32, (USERS, C), 1) + chunk * C
        weighted = jnp.where(position < limit[...], predict - block, 0.0) * confidence[...]
        return split(weighted), items_pair

    def update_items(stratum, chunk, weighted_pair, users_pair):
        rows = pl.ds(chunk * C, C)
        items = held[stratum, rows, :]
        change = product(weighted_pair, users_pair, ((0,), (0,)))
        leaving[stratum, rows, :] = items - learn_rate * (change + penalty * items)

    def add_gradient(chunk, weighted_pair, items_pair):
        part = product(weighted_pair, items_pair, ((1,), (0,)))
        gradient[...] = part if chunk == 0 else gradient[...] + part

    def next_users():
        old = users[...]
        return old - learn_rate * (gradient[...] + penalty * old)

    def one_stratum(stratum, carry):
        rated_load(stratum).wait()
        for chunk in range(CHUNKS):

            @pl.when(stratum > 0)
            def _():
                item_copy(stratum - 1, chunk).wait_recv()

            weighted_pair, items_pair = weigh(stratum, chunk)
            update_items(stratum, chunk, weighted_pair, (users_high[...], users_low[...]))
            item_copy(stratum, chunk).start()
            add_gradient(chunk, weighted_pair, items_pair)
            if chunk == 0:
                rated_load(stratum + 1).start()
        new = next_users()
        users[...] = new
        users_high[...], users_low[...] = split(new)
        prepare(stratum + 1)

        @pl.when(stratum == 0)
        def _():
            row = lax.broadcasted_iota(jnp.int32, (USERS, REFRESH), 0)
            chosen[...] = (row == ids[...]).astype(F32).T.astype(BF16)

        return carry

    lax.fori_loop(0, STRATA - 1, one_stratum, 0)

    final = STRATA - 1
    rated_load(final).wait()
    waiting = []
    for chunk in range(CHUNKS):
        item_copy(final - 1, chunk).wait_recv()
        weighted_pair, items_pair = weigh(final, chunk)
        if chunk < CHUNKS - HOLD:
            update_items(final, chunk, weighted_pair, (users_high[...], users_low[...]))
            last_item_copy(chunk).start()
        else:
            waiting.append((chunk, weighted_pair))
        add_gradient(chunk, weighted_pair, items_pair)
    new = next_users()
    high, low = split(new)
    lowest = (new - high.astype(F32) - low.astype(F32)).astype(BF16)
    pick = functools.partial(lax.dot_general, dimension_numbers=(((1,), (0,)), ((), ())), preferred_element_type=F32)
    picked[wide] = pick(chosen[...], high) + (pick(chosen[...], low) + pick(chosen[...], lowest))

    sent = []

    def piece(slot, half):
        return picked.at[slot] if half is None else picked.at[slot, pl.ds(half * HALF, HALF)]

    def move(slot, half, kind, peer, number):
        return pltpu.make_async_remote_copy(
            src_ref=piece(slot, half),
            dst_ref=piece(slot, half),
            send_sem=pick_send.at[number],
            recv_sem=pick_recv.at[kind],
            device_id=peer,
            device_id_type=MESH,
        )

    def give(slot, half, kind, peer):
        copy = move(slot, half, kind, peer, len(sent))
        copy.start()
        sent.append(copy)

    def take(slot, half, kind):
        move(slot, half, kind, other_core, 0).wait_recv()

    def other_y_kind(half):
        return half

    def near_kind(v, from_up, half):
        return 2 + (v * 2 + from_up) * 2 + half

    def far_kind(v, half):
        return 10 + v * 2 + half

    def core_kind(order):
        return 14 + order

    for half in (0, 1):
        give(wide, half, other_y_kind(half), other_y)
        give(wide, half, near_kind(0, 0, half), x_up)
        give(wide, half, near_kind(0, 1, half), x_down)
    give(wide, None, core_kind(0), other_core)

    for chunk, weighted_pair in waiting:
        update_items(final, chunk, weighted_pair, (users_high[...], users_low[...]))
        last_item_copy(chunk).start()
    users_out[...] = new

    beside = place(0, True, False)
    down, up = place(3, False, False), place(1, False, False)
    beside_down, beside_up = place(3, True, False), place(1, True, False)
    for half in (0, 1):
        take(beside, half, other_y_kind(half))
        give(beside, half, near_kind(1, 0, half), x_up)
        give(beside, half, near_kind(1, 1, half), x_down)
        take(down, half, near_kind(0, 0, half))
        if half == 0:
            give(down, 0, far_kind(0, 0), x_up)
        take(up, half, near_kind(0, 1, half))
        if half == 1:
            give(up, 1, far_kind(0, 1), x_down)
    give(beside, None, core_kind(1), other_core)
    give(down, None, core_kind(2), other_core)
    give(up, None, core_kind(3), other_core)
    for half in (0, 1):
        take(beside_down, half, near_kind(1, 0, half))
        if half == 0:
            give(beside_down, 0, far_kind(1, 0), x_up)
        take(beside_up, half, near_kind(1, 1, half))
        if half == 1:
            give(beside_up, 1, far_kind(1, 1), x_down)
    give(beside_down, None, core_kind(4), other_core)
    give(beside_up, None, core_kind(5), other_core)
    for v in (0, 1):
        opposite = place(2, v == 1, False)
        for half in (0, 1):
            take(opposite, half, far_kind(v, half))
            give(opposite, half, core_kind(6 + 2 * v + half), other_core)

    for chunk in range(CHUNKS):
        last_item_copy(chunk).wait_recv()

    for order, slot in enumerate(
        (
            place(0, False, True), place(0, True, True),
            place(3, False, True), place(1, False, True),
            place(3, True, True), place(1, True, True),
        )
    ):
        take(slot, None, core_kind(order))
    for v in (0, 1):
        for half in (0, 1):
            take(place(2, v == 1, True), half, core_kind(6 + 2 * v + half))

    def drain(stratum, carry):
        for chunk in range(CHUNKS):
            item_copy(stratum, chunk).wait_send()
        return carry

    lax.fori_loop(0, STRATA - 1, drain, 0)
    for chunk in range(CHUNKS):
        last_item_copy(chunk).wait_send()
    for copy in sent:
        copy.wait_send()


def run_strata(ratings, caps, users, items, ids):
    sends, kinds = 27, 24
    far, here = pl.BlockSpec(memory_space=pltpu.HBM), pl.BlockSpec(memory_space=pltpu.VMEM)
    return pl.pallas_call(
        strata_kernel,
        out_shape=(
            jax.ShapeDtypeStruct((USERS, RANK), F32),
            jax.ShapeDtypeStruct((BLOCK, RANK), F32),
            jax.ShapeDtypeStruct((N_WIDE, REFRESH, RANK), F32),
        ),
        in_specs=[far, far, far, far, here],
        out_specs=(here, here, here),
        scratch_shapes=[
            pltpu.VMEM((STRATA, USERS, BLOCK), BF16),
            pltpu.VMEM((STRATA, USERS), jnp.int32),
            pltpu.VMEM((USERS, STRATA), jnp.int32),
            pltpu.VMEM((USERS, RANK), F32),
            pltpu.VMEM((USERS, RANK), BF16),
            pltpu.VMEM((USERS, RANK), BF16),
            pltpu.VMEM((USERS, RANK), F32),
            pltpu.VMEM((STRATA, BLOCK, RANK), F32),
            pltpu.VMEM((STRATA, BLOCK, RANK), F32),
            pltpu.VMEM((REFRESH, USERS), BF16),
            pltpu.VMEM((USERS, C), jnp.int32),
            pltpu.VMEM((USERS, C), F32),
            pltpu.SemaphoreType.DMA((3,)),
            pltpu.SemaphoreType.DMA((STRATA,)),
            pltpu.SemaphoreType.DMA((STRATA, CHUNKS)),
            pltpu.SemaphoreType.DMA((STRATA - 1, CHUNKS)),
            pltpu.SemaphoreType.DMA((CHUNKS,)),
            pltpu.SemaphoreType.DMA((sends,)),
            pltpu.SemaphoreType.DMA((kinds,)),
        ],
        compiler_params=pltpu.CompilerParams(
            collective_id=0, has_side_effects=True, vmem_limit_bytes=VMEM_BYTES
        ),
    )(ratings, caps, users, items, ids)


def scores_kernel(picked, items, users, scores, users_out, items_out, right, staged, store_sem):
    passed = [
        pltpu.make_async_copy(users, users_out, store_sem.at[0]),
        pltpu.make_async_copy(items, items_out, store_sem.at[1]),
    ]
    for copy in passed:
        copy.start()
    high, low = split(items[...].T)
    right[0:RANK, :], right[RANK : 2 * RANK, :], right[2 * RANK :, :] = high, low, high
    stores = []
    for part in range(PARTS):
        rows = pl.ds(part * PART_ROWS, PART_ROWS)
        high, low = split(picked[rows, :])
        left = jnp.concatenate([high, high, low], axis=1)
        staged[rows, :] = jnp.dot(left, right[...], preferred_element_type=F32)
        copy = pltpu.make_async_copy(staged.at[rows], scores.at[rows], store_sem.at[2 + part])
        copy.start()
        stores.append(copy)
    for copy in passed + stores:
        copy.wait()


def run_scores(picked, users, items):
    here = pl.BlockSpec(memory_space=pltpu.VMEM)
    anywhere = pl.BlockSpec(memory_space=pl.ANY)
    return pl.pallas_call(
        scores_kernel,
        out_shape=(
            jax.ShapeDtypeStruct((N_WIDE * REFRESH, BLOCK), F32),
            jax.ShapeDtypeStruct((USERS, RANK), F32),
            jax.ShapeDtypeStruct((BLOCK, RANK), F32),
        ),
        in_specs=[here, here, here],
        out_specs=(anywhere, anywhere, anywhere),
        scratch_shapes=[
            pltpu.VMEM((3 * RANK, BLOCK), BF16),
            pltpu.VMEM((N_WIDE * REFRESH, BLOCK), F32),
            pltpu.SemaphoreType.DMA((2 + PARTS,)),
        ],
        compiler_params=pltpu.CompilerParams(vmem_limit_bytes=32 * 2**20),
    )(picked, items, users)


def per_device(ratings, recency_caps, user_factors, item_factors, refresh_ids):
    inputs = (ratings, recency_caps.T, user_factors, item_factors, refresh_ids.reshape(1, REFRESH))
    inputs = [pltpu.with_memory_space_constraint(value, pltpu.HBM) for value in inputs]
    users, items, picked = run_strata(*inputs)
    scores, users, items = run_scores(picked.reshape(N_WIDE * REFRESH, RANK), users, items)
    return (users, items, scores[None])


def solution(mesh):
    placed = (
        P(("wide", "deep"), None),
        P(("wide", "deep"), None),
        P(("wide", "deep"), None),
        P(("wide", "deep"), None),
        P(("wide", "deep")),
    )
    return jax.shard_map(
        per_device,
        mesh=mesh,
        in_specs=placed,
        out_specs=(P(("wide", "deep"), None), P(("wide", "deep"), None), P("deep", None, "wide")),
        check_vma=False,
    )
```

```python
import functools

import jax
import jax.numpy as jnp
from jax import lax
from jax.experimental import pallas as pl
from jax.experimental.pallas import tpu as pltpu
from jax.sharding import PartitionSpec as P

STRATA = 8
USERS = 512
BLOCK = 512
RANK = 256
REFRESH = 128
N_WIDE = 16
N_DEEP = 16
X = 4
CHUNKS = 4
C = BLOCK // CHUNKS

VMEM_BYTES = 44 * 2**20
PARTS = 8
HOLD = 2
HALF = REFRESH // 2
PART_ROWS = N_WIDE * REFRESH // PARTS

learn_rate = 0.1
penalty = 0.05

MESH = pl.DeviceIdType.MESH
F32 = jnp.float32
BF16 = jnp.bfloat16


def split(value):
    high = value.astype(BF16)
    return high, (value - high.astype(F32)).astype(BF16)


def product(left, right, dims):
    numbers = ((dims[0], dims[1]), ((), ()))
    dot = functools.partial(lax.dot_general, dimension_numbers=numbers, preferred_element_type=F32)
    return dot(left[0], right[0]) + (dot(left[0], right[1]) + dot(left[1], right[0]))


def strata_kernel(
    ratings, caps_in, users_in, items_in, ids,
    users_out, items_out, picked_high, picked_low, right,
    rated, caps_across, caps, users, users_high, users_low, gradient, held, leaving, chosen, picked, limit, confidence,
    load_sem, rated_sem, item_send, item_recv, last_recv, pick_send, pick_recv,
):
    wide, deep = lax.axis_index("wide"), lax.axis_index("deep")
    joined = wide * N_DEEP + deep
    after = lax.rem(joined + 1, N_WIDE * N_DEEP)
    before = lax.rem(joined + N_WIDE * N_DEEP - 1, N_WIDE * N_DEEP)
    after = (after // N_DEEP, lax.rem(after, N_DEEP))
    before = (before // N_DEEP, lax.rem(before, N_DEEP))

    x, y_low, core = wide // 4, lax.rem(wide // 2, 2), lax.rem(wide, 2)

    def place(x_by, y_flip, core_flip):
        return lax.rem(x + x_by, X) * 4 + (1 - y_low if y_flip else y_low) * 2 + (1 - core if core_flip else core)

    other_core = (place(0, False, True), deep)
    other_y = (place(0, True, False), deep)
    x_up = (place(1, False, False), deep)
    x_down = (place(3, False, False), deep)

    barrier = pltpu.get_barrier_semaphore()
    for peer in (after, before, other_core, other_y, x_up, x_down):
        pl.semaphore_signal(barrier, inc=1, device_id=peer, device_id_type=MESH)

    loads = [
        pltpu.make_async_copy(users_in, users, load_sem.at[0]),
        pltpu.make_async_copy(items_in, held.at[0], load_sem.at[1]),
        pltpu.make_async_copy(caps_in, caps_across, load_sem.at[2]),
    ]
    for load in loads:
        load.start()

    def rated_load(stratum):
        columns = pl.ds(pl.multiple_of(stratum * BLOCK, BLOCK), BLOCK)
        return pltpu.make_async_copy(ratings.at[:, columns], rated.at[stratum], rated_sem.at[stratum])

    rated_load(0).start()

    def item_copy(stratum, chunk):
        rows = pl.ds(chunk * C, C)
        return pltpu.make_async_remote_copy(
            src_ref=leaving.at[stratum, rows],
            dst_ref=held.at[stratum + 1, rows],
            send_sem=item_send.at[stratum, chunk],
            recv_sem=item_recv.at[stratum, chunk],
            device_id=after,
            device_id_type=MESH,
        )

    def last_item_copy(chunk):
        rows = pl.ds(chunk * C, C)
        return pltpu.make_async_remote_copy(
            src_ref=leaving.at[STRATA - 1, rows],
            dst_ref=items_out.at[rows],
            send_sem=item_send.at[STRATA - 1, chunk],
            recv_sem=last_recv.at[chunk],
            device_id=after,
            device_id_type=MESH,
        )

    def prepare(stratum):
        lane = lax.broadcasted_iota(jnp.int32, (USERS, STRATA), 1)
        column = jnp.sum(jnp.where(lane == stratum, caps[...], 0), axis=1, keepdims=True)
        limit[...] = jnp.broadcast_to(column, (USERS, C))

    loads[2].wait()
    caps[...] = caps_across[...].T
    counts = jnp.sum(caps[...], axis=1, keepdims=True).astype(F32)
    confidence[...] = jnp.broadcast_to(lax.rsqrt(counts), (USERS, C))
    loads[0].wait()
    users_high[...], users_low[...] = split(users[...])
    loads[1].wait()

    prepare(0)
    pl.semaphore_wait(barrier, 6)

    def weigh(stratum, chunk):
        rows = pl.ds(chunk * C, C)
        items_pair = split(held[stratum, rows, :])
        predict = product((users_high[...], users_low[...]), items_pair, ((1,), (1,)))
        block = rated[stratum, :, rows].astype(F32)
        position = lax.broadcasted_iota(jnp.int32, (USERS, C), 1) + chunk * C
        weighted = jnp.where(position < limit[...], predict - block, 0.0) * confidence[...]
        return split(weighted), items_pair

    def update_items(stratum, chunk, weighted_pair, users_pair):
        rows = pl.ds(chunk * C, C)
        items = held[stratum, rows, :]
        change = product(weighted_pair, users_pair, ((0,), (0,)))
        leaving[stratum, rows, :] = items - learn_rate * (change + penalty * items)

    def add_gradient(chunk, weighted_pair, items_pair):
        part = product(weighted_pair, items_pair, ((1,), (0,)))
        gradient[...] = part if chunk == 0 else gradient[...] + part

    def next_users():
        old = users[...]
        return old - learn_rate * (gradient[...] + penalty * old)

    def one_stratum(stratum, carry):
        rated_load(stratum).wait()
        for chunk in range(CHUNKS):

            @pl.when(stratum > 0)
            def _():
                item_copy(stratum - 1, chunk).wait_recv()

            weighted_pair, items_pair = weigh(stratum, chunk)
            update_items(stratum, chunk, weighted_pair, (users_high[...], users_low[...]))
            item_copy(stratum, chunk).start()
            add_gradient(chunk, weighted_pair, items_pair)
            if chunk == 0:
                rated_load(stratum + 1).start()
        new = next_users()
        users[...] = new
        users_high[...], users_low[...] = split(new)
        prepare(stratum + 1)

        @pl.when(stratum == 0)
        def _():
            row = lax.broadcasted_iota(jnp.int32, (USERS, REFRESH), 0)
            chosen[...] = (row == ids[...]).astype(F32).T.astype(BF16)

        return carry

    lax.fori_loop(0, STRATA - 1, one_stratum, 0)

    final = STRATA - 1
    rated_load(final).wait()
    waiting = []
    for chunk in range(CHUNKS):
        item_copy(final - 1, chunk).wait_recv()
        weighted_pair, items_pair = weigh(final, chunk)
        if chunk < CHUNKS - HOLD:
            update_items(final, chunk, weighted_pair, (users_high[...], users_low[...]))
            last_item_copy(chunk).start()
        else:
            waiting.append((chunk, weighted_pair))
        add_gradient(chunk, weighted_pair, items_pair)
    new = next_users()
    high, low = split(new)
    lowest = (new - high.astype(F32) - low.astype(F32)).astype(BF16)
    pick = functools.partial(lax.dot_general, dimension_numbers=(((1,), (0,)), ((), ())), preferred_element_type=F32)
    picked[wide] = pick(chosen[...], high) + (pick(chosen[...], low) + pick(chosen[...], lowest))

    sent = []

    def piece(slot, half):
        return picked.at[slot] if half is None else picked.at[slot, pl.ds(half * HALF, HALF)]

    def move(slot, half, kind, peer, number):
        return pltpu.make_async_remote_copy(
            src_ref=piece(slot, half),
            dst_ref=piece(slot, half),
            send_sem=pick_send.at[number],
            recv_sem=pick_recv.at[kind],
            device_id=peer,
            device_id_type=MESH,
        )

    def give(slot, half, kind, peer):
        copy = move(slot, half, kind, peer, len(sent))
        copy.start()
        sent.append(copy)

    def ready(slot, half=None):
        start, length = (0, REFRESH) if half is None else (half * HALF, HALF)
        rows = pl.ds(pl.multiple_of(slot * REFRESH + start, HALF), length)
        picked_high[rows, :], picked_low[rows, :] = split(piece(slot, half)[...])

    def take(slot, half, kind):
        move(slot, half, kind, other_core, 0).wait_recv()

    def other_y_kind(half):
        return half

    def near_kind(v, from_up, half):
        return 2 + (v * 2 + from_up) * 2 + half

    def far_kind(v, half):
        return 10 + v * 2 + half

    def core_kind(order):
        return 14 + order

    for half in (0, 1):
        give(wide, half, other_y_kind(half), other_y)
        give(wide, half, near_kind(0, 0, half), x_up)
        give(wide, half, near_kind(0, 1, half), x_down)
    give(wide, None, core_kind(0), other_core)

    for chunk, weighted_pair in waiting:
        update_items(final, chunk, weighted_pair, (users_high[...], users_low[...]))
        last_item_copy(chunk).start()
    users_out[...] = new
    ready(wide)

    beside = place(0, True, False)
    down, up = place(3, False, False), place(1, False, False)
    beside_down, beside_up = place(3, True, False), place(1, True, False)
    for half in (0, 1):
        take(beside, half, other_y_kind(half))
        give(beside, half, near_kind(1, 0, half), x_up)
        give(beside, half, near_kind(1, 1, half), x_down)
        take(down, half, near_kind(0, 0, half))
        if half == 0:
            give(down, 0, far_kind(0, 0), x_up)
        take(up, half, near_kind(0, 1, half))
        if half == 1:
            give(up, 1, far_kind(0, 1), x_down)
    give(beside, None, core_kind(1), other_core)
    give(down, None, core_kind(2), other_core)
    give(up, None, core_kind(3), other_core)
    ready(beside)
    ready(down)
    ready(up)
    for half in (0, 1):
        take(beside_down, half, near_kind(1, 0, half))
        if half == 0:
            give(beside_down, 0, far_kind(1, 0), x_up)
        take(beside_up, half, near_kind(1, 1, half))
        if half == 1:
            give(beside_up, 1, far_kind(1, 1), x_down)
    give(beside_down, None, core_kind(4), other_core)
    give(beside_up, None, core_kind(5), other_core)
    ready(beside_down)
    ready(beside_up)
    for v in (0, 1):
        opposite = place(2, v == 1, False)
        for half in (0, 1):
            take(opposite, half, far_kind(v, half))
            give(opposite, half, core_kind(6 + 2 * v + half), other_core)
            ready(opposite, half)

    for chunk in range(CHUNKS):
        last_item_copy(chunk).wait_recv()
        columns = pl.ds(chunk * C, C)
        high, low = split(items_out[columns, :].T)
        right[0:RANK, columns], right[RANK : 2 * RANK, columns], right[2 * RANK :, columns] = high, low, high

    for order, slot in enumerate(
        (
            place(0, False, True), place(0, True, True),
            place(3, False, True), place(1, False, True),
            place(3, True, True), place(1, True, True),
        )
    ):
        take(slot, None, core_kind(order))
        ready(slot)
    for v in (0, 1):
        for half in (0, 1):
            take(place(2, v == 1, True), half, core_kind(6 + 2 * v + half))
            ready(place(2, v == 1, True), half)

    def drain(stratum, carry):
        for chunk in range(CHUNKS):
            item_copy(stratum, chunk).wait_send()
        return carry

    lax.fori_loop(0, STRATA - 1, drain, 0)
    for chunk in range(CHUNKS):
        last_item_copy(chunk).wait_send()
    for copy in sent:
        copy.wait_send()


def run_strata(ratings, caps, users, items, ids):
    sends, kinds = 27, 24
    far, here = pl.BlockSpec(memory_space=pltpu.HBM), pl.BlockSpec(memory_space=pltpu.VMEM)
    return pl.pallas_call(
        strata_kernel,
        out_shape=(
            jax.ShapeDtypeStruct((USERS, RANK), F32),
            jax.ShapeDtypeStruct((BLOCK, RANK), F32),
            jax.ShapeDtypeStruct((N_WIDE * REFRESH, RANK), BF16),
            jax.ShapeDtypeStruct((N_WIDE * REFRESH, RANK), BF16),
            jax.ShapeDtypeStruct((3 * RANK, BLOCK), BF16),
        ),
        in_specs=[far, far, far, far, here],
        out_specs=(here,) * 5,
        scratch_shapes=[
            pltpu.VMEM((STRATA, USERS, BLOCK), BF16),
            pltpu.VMEM((STRATA, USERS), jnp.int32),
            pltpu.VMEM((USERS, STRATA), jnp.int32),
            pltpu.VMEM((USERS, RANK), F32),
            pltpu.VMEM((USERS, RANK), BF16),
            pltpu.VMEM((USERS, RANK), BF16),
            pltpu.VMEM((USERS, RANK), F32),
            pltpu.VMEM((STRATA, BLOCK, RANK), F32),
            pltpu.VMEM((STRATA, BLOCK, RANK), F32),
            pltpu.VMEM((REFRESH, USERS), BF16),
            pltpu.VMEM((N_WIDE, REFRESH, RANK), F32),
            pltpu.VMEM((USERS, C), jnp.int32),
            pltpu.VMEM((USERS, C), F32),
            pltpu.SemaphoreType.DMA((3,)),
            pltpu.SemaphoreType.DMA((STRATA,)),
            pltpu.SemaphoreType.DMA((STRATA, CHUNKS)),
            pltpu.SemaphoreType.DMA((STRATA - 1, CHUNKS)),
            pltpu.SemaphoreType.DMA((CHUNKS,)),
            pltpu.SemaphoreType.DMA((sends,)),
            pltpu.SemaphoreType.DMA((kinds,)),
        ],
        compiler_params=pltpu.CompilerParams(
            collective_id=0, has_side_effects=True, vmem_limit_bytes=VMEM_BYTES
        ),
    )(ratings, caps, users, items, ids)


def scores_kernel(picked_high, picked_low, right, items, users, scores, users_out, items_out, staged, store_sem):
    passed = [
        pltpu.make_async_copy(users, users_out, store_sem.at[0]),
        pltpu.make_async_copy(items, items_out, store_sem.at[1]),
    ]
    for copy in passed:
        copy.start()
    stores = []
    for part in range(PARTS):
        rows = pl.ds(part * PART_ROWS, PART_ROWS)
        high, low = picked_high[rows, :], picked_low[rows, :]
        left = jnp.concatenate([high, high, low], axis=1)
        staged[rows, :] = jnp.dot(left, right[...], preferred_element_type=F32)
        copy = pltpu.make_async_copy(staged.at[rows], scores.at[rows], store_sem.at[2 + part])
        copy.start()
        stores.append(copy)
    for copy in passed + stores:
        copy.wait()


def run_scores(picked_high, picked_low, right, users, items):
    here = pl.BlockSpec(memory_space=pltpu.VMEM)
    anywhere = pl.BlockSpec(memory_space=pl.ANY)
    return pl.pallas_call(
        scores_kernel,
        out_shape=(
            jax.ShapeDtypeStruct((N_WIDE * REFRESH, BLOCK), F32),
            jax.ShapeDtypeStruct((USERS, RANK), F32),
            jax.ShapeDtypeStruct((BLOCK, RANK), F32),
        ),
        in_specs=[here] * 5,
        out_specs=(anywhere, anywhere, anywhere),
        scratch_shapes=[
            pltpu.VMEM((N_WIDE * REFRESH, BLOCK), F32),
            pltpu.SemaphoreType.DMA((2 + PARTS,)),
        ],
        compiler_params=pltpu.CompilerParams(vmem_limit_bytes=32 * 2**20),
    )(picked_high, picked_low, right, items, users)


def per_device(ratings, recency_caps, user_factors, item_factors, refresh_ids):
    inputs = (ratings, recency_caps.T, user_factors, item_factors, refresh_ids.reshape(1, REFRESH))
    inputs = [pltpu.with_memory_space_constraint(value, pltpu.HBM) for value in inputs]
    users, items, picked_high, picked_low, right = run_strata(*inputs)
    scores, users, items = run_scores(picked_high, picked_low, right, users, items)
    return (users, items, scores[None])


def solution(mesh):
    placed = (
        P(("wide", "deep"), None),
        P(("wide", "deep"), None),
        P(("wide", "deep"), None),
        P(("wide", "deep"), None),
        P(("wide", "deep")),
    )
    return jax.shard_map(
        per_device,
        mesh=mesh,
        in_specs=placed,
        out_specs=(P(("wide", "deep"), None), P(("wide", "deep"), None), P("deep", None, "wide")),
        check_vma=False,
    )
```
